32 devices in a mesh: groups: 2 (over x), owner: 16 (over z, y, core).
Axes of the slice: x: 2, y: 2, z: 4, core: 2. Of those that a mesh axis runs over, the one named last changes fastest.
Arguments:
- features: bfloat16 [16384, 1024], P(('groups', 'owner')), parts along dimension 0, may hold values from -6 to 6
- history: bfloat16 [2, 32768, 1024], P(None, ('groups', 'owner')), parts along dimension 1, may hold values from -6 to 6
- weights: bfloat16 [2, 1024, 1024], replicated, may hold values from -0.1875 to 0.1875
- edge_weights: float32 [16384, 768], P(('groups', 'owner')), parts along dimension 0, may hold values from 0 to 10, as said below
- requests: int32 [32, 16, 16], P(('groups', 'owner')), parts along dimension 0, may hold values from 0 to 1023, as said below
- counts: int32 [32, 16], P(('groups', 'owner')), parts along dimension 0, may hold values from 1 to 16, as said below
- push_slots: int32 [32, 512], P(('groups', 'owner')), parts along dimension 0, may hold values from 0 to 1023, as said below
- cotangent: bfloat16 [16384, 1024], P(('groups', 'owner')), parts along dimension 0, may hold values from -6 to 6
Outputs:
- result: bfloat16 [16384, 1024], P(('groups', 'owner')), parts along dimension 0
- new_history: bfloat16 [1, 32768, 1024], P(None, ('groups', 'owner')), parts along dimension 1
- weight_grads: float32 [4, 1024, 1024], P('groups'), parts along dimension 0
The draws below stay inside these ranges and needn't reach their ends.
There are 2 independent parts, one for each index of `groups`. The reference program is written for one: setup_inputs(seed, part) draws one part's arguments, and reference() takes and returns one part's arrays. A program takes and returns all parts, laid end to end along the dimension named above; an argument that names none is the same for every part. Nothing has to cross between parts.
Inputs may be any that keep to these rules, and one draw needn't show every extreme that they name: `requests`: every entry, padding slots too, names a row of that owner outside the rows in push_slots. `counts`: some owner has all 16 slots used by every device. `push_slots`: each owner's row holds distinct local rows. `edge_weights`: Nonnegative; the entry of each batch node's own column is positive.
All inputs are finite; a program needn't handle non-finite values.
Results may differ from the reference program's by a relative error of at most 0.0038.
The reference program's roundings to bfloat16 on the way count: a program that leaves them out, or rounds other values in their place, can miss the bound.
Values may be sent and summed in bfloat16 or wider, within the bound.
A program may use at most 128 MiB of HBM per device.

```python
import math
import jax
import jax.numpy as jnp
from jax import lax

H = 1024
LAYERS = 2
NB = 512
HIST_DEV = 1024
CAP = 16
NODES = 8192
HROWS = 16384
N_OWNER = 16


def owner_orders(key):
    split_keys = jax.random.split(key, N_OWNER)
    orders = jax.vmap(lambda one_key: jax.random.permutation(one_key, HIST_DEV))(split_keys)
    return orders.astype(jnp.int32)


def draw_push_slots(key, part):
    orders = owner_orders(key)
    return orders[:, :NB]


def draw_requests(key, part):
    orders = owner_orders(key)
    key = jax.random.fold_in(key, 11)
    chosen = jax.random.randint(key, (N_OWNER, N_OWNER, CAP), NB, HIST_DEV, dtype=jnp.int32)
    owner_ids = jnp.arange(N_OWNER, dtype=jnp.int32)[None, :, None]
    return orders[owner_ids, chosen]


def draw_counts(key, part):
    key = jax.random.fold_in(key, 23)
    first_key, second_key, third_key = jax.random.split(key, 3)
    popularity = jax.random.randint(first_key, (N_OWNER,), 1, CAP + 1, dtype=jnp.int32)
    raw_values = jax.random.randint(second_key, (N_OWNER, N_OWNER), 0, 1 << 20, dtype=jnp.int32)
    filled = 1 + raw_values % popularity[None, :]
    busiest = jax.random.randint(third_key, (), 0, N_OWNER, dtype=jnp.int32)
    owner_pos = jnp.arange(N_OWNER, dtype=jnp.int32)[None, :]
    return jnp.where(owner_pos == busiest, CAP, filled).astype(jnp.int32)


def draw_edge_weights(key, part):
    key = jax.random.fold_in(key, 37)
    first_key, second_key = jax.random.split(key)
    columns = NB + CAP * N_OWNER
    total_rows = NB * N_OWNER
    chosen = jax.random.randint(first_key, (total_rows, columns), 0, 32, dtype=jnp.int32) == 0
    magnitude = jnp.exp(jax.random.uniform(second_key, (total_rows, columns), jnp.float32, math.log(0.1), math.log(10.0)))
    row_pos = jnp.arange(total_rows, dtype=jnp.int32)[:, None] % NB
    col_pos = jnp.arange(columns, dtype=jnp.int32)[None, :]
    return jnp.where(chosen | (col_pos == row_pos), magnitude, 0.0).astype(jnp.float32)


def block_levels(stream_key, extent, pieces, least, high):
    factor_of = 1.0
    for axis_at, shards_of in pieces:
        heights = jax.random.uniform(jax.random.fold_in(jax.random.fold_in(stream_key, 6), axis_at), (shards_of,), jnp.float32, least / len(pieces), high / len(pieces))
        factor_of = factor_of * jnp.repeat(jnp.exp(heights), extent[axis_at] // shards_of).reshape((-1,) + (1,) * (len(extent) - 1 - axis_at))
    return factor_of


def centred(stream_key, shape, scale, limit, cuts=(), kind=jnp.bfloat16):
    values = jax.random.normal(stream_key, shape, jnp.float32) * scale
    if len(cuts) > 0:
        values = block_levels(stream_key, shape, cuts, -0.22, 0.18) * values
    return jnp.clip(values, min=-limit, max=limit).astype(kind)


def setup_inputs(seed: int = 0, part: int = 0) -> dict:
    keys = jax.random.split(jax.random.key(seed), 9)
    part_keys = jax.random.split(jax.random.fold_in(keys[8], part), 9)
    return {
        "features": centred(part_keys[0], (NODES, H), 1.0, 6.0, ((0, 16),)),
        "history": centred(part_keys[1], (LAYERS, HROWS, H), 1.0, 6.0, ((1, 16),)),
        "weights": centred(keys[2], (LAYERS, H, H), H ** -0.5, 0.1875),
        "edge_weights": draw_edge_weights(jax.random.fold_in(jax.random.fold_in(keys[8], part), 71), part),
        "requests": draw_requests(jax.random.fold_in(jax.random.fold_in(keys[8], part), 71), part),
        "counts": draw_counts(jax.random.fold_in(jax.random.fold_in(keys[8], part), 71), part),
        "push_slots": draw_push_slots(jax.random.fold_in(jax.random.fold_in(keys[8], part), 71), part),
        "cotangent": centred(part_keys[7], (NODES, H), 1.0, 6.0, ((0, 16),)),
    }


RESIDUAL = 0.1

def strength(layer_no):
    return math.log(0.5 / (layer_no + 1) + 1.0)

def reference(features, history, weights, edge_weights, requests, counts, push_slots, cotangent):
    owners = N_OWNER
    push_rows = NB // owners
    start_rows = features.reshape(owners, NB, H)
    tables = history.reshape(LAYERS, owners, HIST_DEV, H)
    valid_slots = jnp.arange(CAP, dtype=jnp.int32)[None, None, :] < counts[:, :, None]
    valid_slots = valid_slots.reshape(owners, owners * CAP)
    valid_slots = jnp.concatenate([jnp.ones((owners, NB), bool), valid_slots], axis=1)
    masked = edge_weights.reshape(owners, NB, NB + owners * CAP) * valid_slots[:, None, :].astype(jnp.float32)
    norm_adj = (masked / lax.optimization_barrier(jnp.sum(masked, axis=-1, keepdims=True))).astype(jnp.bfloat16)
    owner_ids = jnp.arange(owners, dtype=jnp.int32)[None, :, None]
    current = start_rows
    supports = []
    pre_list = []
    fresh_tables = []
    for layer_no in range(LAYERS):
        mix_weight = strength(layer_no)
        pulled = tables[layer_no][owner_ids, requests].reshape(owners, owners * CAP, H)
        neighbours = jnp.concatenate([current, pulled], axis=1)
        gathered_sum = jnp.einsum('gij,gjh->gih', norm_adj.astype(jnp.float32), neighbours.astype(jnp.float32))
        support = ((1.0 - RESIDUAL) * gathered_sum + RESIDUAL * start_rows.astype(jnp.float32)).astype(jnp.bfloat16)
        linear_part = jnp.dot(support.reshape(-1, H), weights[layer_no], preferred_element_type=jnp.float32).reshape(owners, NB, H)
        pre_relu = (1.0 - mix_weight) * support.astype(jnp.float32) + mix_weight * linear_part
        current = jnp.maximum(pre_relu, 0.0).astype(jnp.bfloat16)
        supports.append(support)
        pre_list.append(pre_relu)
        if layer_no + 1 < LAYERS:
            pushed = current.reshape(owners, owners, push_rows, H).transpose(1, 0, 2, 3).reshape(owners, NB, H)
            row_ids = jnp.arange(owners, dtype=jnp.int32)[:, None]
            fresh = tables[layer_no + 1].at[row_ids, push_slots].set(pushed)
            fresh_tables.append(fresh.reshape(owners * HIST_DEV, H))
    grad_scale = 1.0 / math.sqrt(owners * NB)
    weight_terms = [None] * LAYERS
    upstream = cotangent.reshape(owners, NB, H).astype(jnp.float32)
    for layer_no in reversed(range(LAYERS)):
        mix_weight = strength(layer_no)
        gate_grad = jnp.where(pre_list[layer_no] > 0, upstream, 0.0).astype(jnp.bfloat16)
        flat_support = supports[layer_no].reshape(-1, H)
        flat_gate = gate_grad.reshape(-1, H)
        weight_terms[layer_no] = mix_weight * grad_scale * jnp.dot(flat_support.T, flat_gate, preferred_element_type=jnp.float32)
        if layer_no > 0:
            through_weight = jnp.dot(flat_gate, weights[layer_no].T, preferred_element_type=jnp.float32).reshape(owners, NB, H)
            support_grad = ((1.0 - mix_weight) * gate_grad.astype(jnp.float32) + mix_weight * through_weight).astype(jnp.bfloat16)
            upstream = (1.0 - RESIDUAL) * jnp.einsum('gij,gih->gjh', norm_adj[:, :, :NB].astype(jnp.float32), support_grad.astype(jnp.float32))
    result = current.reshape(owners * NB, H)
    return (result, jnp.stack(fresh_tables), jnp.stack(weight_terms))
```

```python
import functools
import math

import jax
import jax.numpy as jnp
from jax import lax
from jax.experimental import pallas as pl
from jax.experimental.pallas import tpu as pltpu
from jax.sharding import PartitionSpec as P

RESIDUAL = 0.1
MESH = pl.DeviceIdType.MESH
TILE = 256
ROWS = 16
MIB = 1 << 20


def strength(layer_no):
    return math.log(0.5 / (layer_no + 1) + 1.0)


def ds(start, size, unit=ROWS):
    return pl.ds(pl.multiple_of(start, unit), size)


def dot(a, b, dims=((1,), (0,))):
    return lax.dot_general(a, b, (dims, ((), ())), preferred_element_type=jnp.float32)


def step_kernel(
    owners, slots, grad_scale,
    feat, hist, weights, edge, valid, req, cot,
    grads_out, incoming_out, result_out,
    req_in, onehot, served, pulled, adj, sup, gate, cur1, back, result, incoming,
    acc, sent, got, full,
    req_send, req_recv, pull_send, pull_recv, push_send, push_recv, ar_send, ar_recv, out_sem,
):
    me = lax.axis_index("owner")
    batch, hidden = feat.shape
    hist_rows = hist.shape[1]
    push = batch // owners
    steps = owners.bit_length() - 1
    size = ROWS * owners
    half = hidden // size
    chunks = 2 * half
    blocks = hidden // TILE

    barrier = pltpu.get_barrier_semaphore()

    def greet(p, c):
        pl.semaphore_signal(
            barrier, inc=1, device_id={"owner": lax.rem(me + p, owners)}, device_id_type=MESH
        )
        return c

    lax.fori_loop(1, owners, greet, 0)
    pl.semaphore_wait(barrier, owners - 1)

    def req_copy(p):
        peer = lax.rem(me + p, owners)
        return pltpu.make_async_remote_copy(
            src_ref=req.at[peer], dst_ref=req_in.at[me],
            send_sem=req_send.at[p], recv_sem=req_recv.at[p],
            device_id={"owner": peer}, device_id_type=MESH,
        )

    def each_peer(fn):
        def run(p, c):
            fn(p)
            return c

        lax.fori_loop(1, owners, run, 0)

    each_peer(lambda p: req_copy(p).start())
    req_in[me] = req[me]

    def norm_rows(i, c):
        rows = ds(i * 32, 32, 32)
        masked = edge[rows, :] * valid[...]
        adj[rows, :] = (masked / jnp.sum(masked, axis=1, keepdims=True)).astype(jnp.bfloat16)
        return c

    lax.fori_loop(0, batch // 32, norm_rows, 0)
    each_peer(lambda p: req_copy(p).wait())

    def pick_rows(o, c):
        rows = ds(o * slots, slots)
        want = req_in[o]
        for j in range(hist_rows // 128):
            lanes = lax.broadcasted_iota(jnp.int32, (slots, 128), 1) + j * 128
            onehot[rows, j * 128:(j + 1) * 128] = jnp.where(lanes == want, 1.0, 0.0).astype(
                jnp.bfloat16
            )
        return c

    lax.fori_loop(0, owners, pick_rows, 0)

    def pull_copy(layer_no, p):
        peer = lax.rem(me + p, owners)
        return pltpu.make_async_remote_copy(
            src_ref=served.at[layer_no, ds(peer * slots, slots)],
            dst_ref=pulled.at[layer_no, ds(me * slots, slots)],
            send_sem=pull_send.at[layer_no, p], recv_sem=pull_recv.at[layer_no, p],
            device_id={"owner": peer}, device_id_type=MESH,
        )

    for layer_no in range(2):
        def serve(j, c, layer_no=layer_no):
            cols = ds(j * TILE, TILE, TILE)
            served[layer_no, :, cols] = dot(onehot[...], hist[layer_no, :, cols]).astype(jnp.bfloat16)
            return c

        lax.fori_loop(0, blocks, serve, 0)
        each_peer(lambda p, layer_no=layer_no: pull_copy(layer_no, p).start())
        pulled[layer_no, ds(me * slots, slots), :] = served[layer_no, ds(me * slots, slots), :]

    def push_copy(p):
        peer = lax.rem(me + p, owners)
        return pltpu.make_async_remote_copy(
            src_ref=cur1.at[ds(peer * push, push)],
            dst_ref=incoming.at[ds(me * push, push)],
            send_sem=push_send.at[p], recv_sem=push_recv.at[p],
            device_id={"owner": peer}, device_id_type=MESH,
        )

    for layer_no in range(2):
        mix = strength(layer_no)
        source = feat if layer_no == 0 else cur1

        def own_sum(j, c, source=source):
            cols = ds(j * TILE, TILE, TILE)
            back[:, cols] = dot(adj[:, :batch], source[:, cols])
            return c

        lax.fori_loop(0, blocks, own_sum, 0)
        each_peer(lambda p, layer_no=layer_no: pull_copy(layer_no, p).wait())

        def far_sum(j, c, layer_no=layer_no):
            cols = ds(j * TILE, TILE, TILE)
            total = back[:, cols] + dot(adj[:, batch:], pulled[layer_no, :, cols])
            sup[layer_no, :, cols] = (
                (1.0 - RESIDUAL) * total + RESIDUAL * feat[:, cols].astype(jnp.float32)
            ).astype(jnp.bfloat16)
            return c

        lax.fori_loop(0, blocks, far_sum, 0)

        def linear(j, c, layer_no=layer_no, mix=mix):
            cols = ds(j * TILE, TILE, TILE)
            pre = (1.0 - mix) * sup[layer_no, :, cols].astype(jnp.float32) + mix * dot(
                sup[layer_no], weights[layer_no, :, cols]
            )
            out = jnp.maximum(pre, 0.0).astype(jnp.bfloat16)
            if layer_no == 0:
                cur1[:, cols] = out
            else:
                result[:, cols] = out
                gate[1, :, cols] = jnp.where(
                    pre > 0, cot[:, cols].astype(jnp.float32), 0.0
                ).astype(jnp.bfloat16)
            return c

        lax.fori_loop(0, blocks, linear, 0)
        if layer_no == 0:
            each_peer(lambda p: push_copy(p).start())
            incoming[ds(me * push, push), :] = cur1[ds(me * push, push), :]

    result_copy = pltpu.make_async_copy(result, result_out, out_sem.at[chunks])
    result_copy.start()

    def backward():
        mix = strength(1)

        def through(j, c):
            cols = ds(j * TILE, TILE, TILE)
            value = (1.0 - mix) * gate[1, :, cols].astype(jnp.float32) + mix * dot(
                gate[1], weights[1, cols, :], ((1,), (1,))
            )
            gate[0, :, cols] = value.astype(jnp.bfloat16)
            return c

        lax.fori_loop(0, blocks, through, 0)

        def up(j, c):
            cols = ds(j * TILE, TILE, TILE)
            upstream = (1.0 - RESIDUAL) * dot(adj[:, :batch], gate[0, :, cols], ((0,), (0,)))
            gate[0, :, cols] = jnp.where(
                cur1[:, cols].astype(jnp.float32) > 0, upstream, 0.0
            ).astype(jnp.bfloat16)
            return c

        lax.fori_loop(0, blocks, up, 0)

    bits = [lax.rem(me // (1 << b), 2) for b in range(steps)]
    peers = [me + (1 - 2 * bits[b]) * (1 << b) for b in range(steps)]
    width = [size >> (b + 1) for b in range(steps)]
    start = [0]
    for b in range(steps):
        start.append(start[-1] + bits[b] * width[b])
    other = [start[b] + (1 - bits[b]) * width[b] for b in range(steps)]
    stage_at = [size - (size >> b) for b in range(steps)]

    def rs_copy(k, b):
        rows = pl.ds(stage_at[b], width[b])
        return pltpu.make_async_remote_copy(
            src_ref=sent.at[k, rows], dst_ref=got.at[k, rows],
            send_sem=ar_send.at[k, b], recv_sem=ar_recv.at[k, b],
            device_id={"owner": peers[b]}, device_id_type=MESH,
        )

    def ag_copy(k, b):
        rows = ds(start[b + 1], width[b])
        return pltpu.make_async_remote_copy(
            src_ref=full.at[k, rows], dst_ref=full.at[k, rows],
            send_sem=ar_send.at[k, steps + b], recv_sem=ar_recv.at[k, steps + b],
            device_id={"owner": peers[b]}, device_id_type=MESH,
        )

    def out_copy(k):
        row = (1 - k // half) * hidden + lax.rem(k, half) * size
        return pltpu.make_async_copy(
            full.at[k], grads_out.at[ds(row, size)], out_sem.at[k]
        )

    def each_row(count, fn):
        def run(i, c):
            fn(i * ROWS)
            return c

        lax.fori_loop(0, count // ROWS, run, 0)

    def stage(k, s):
        if s == 0:
            @pl.when(k == half)
            def _():
                backward()

            layer_no = 1 - k // half
            scale = grad_scale * jnp.where(layer_no == 1, strength(1), strength(0))

            def product(i, c):
                cols = ds(lax.rem(k, half) * size + i * TILE, TILE, TILE)
                acc[k, ds(i * TILE, TILE, TILE), :] = scale * dot(
                    sup[layer_no, :, cols], gate[layer_no], ((0,), (0,))
                )
                return c

            lax.fori_loop(0, size // TILE, product, 0)

            def pack(i):
                sent[k, ds(i, ROWS), :] = acc[k, ds(other[0] + i, ROWS), :].astype(jnp.bfloat16)

            each_row(width[0], pack)
            rs_copy(k, 0).start()
        elif s < steps:
            rs_copy(k, s - 1).wait_recv()
            base = stage_at[s - 1]

            def pack(i):
                total = acc[k, ds(other[s] + i, ROWS), :] + got[
                    k, ds(base + (1 - bits[s]) * width[s] + i, ROWS), :
                ].astype(jnp.float32)
                sent[k, ds(stage_at[s] + i, ROWS), :] = total.astype(jnp.bfloat16)

            each_row(width[s], pack)
            rs_copy(k, s).start()

            def keep(i):
                rows = ds(start[s + 1] + i, ROWS)
                acc[k, rows, :] = acc[k, rows, :] + got[
                    k, ds(base + bits[s] * width[s] + i, ROWS), :
                ].astype(jnp.float32)

            each_row(width[s], keep)
        elif s == steps:
            rs_copy(k, s - 1).wait_recv()
            rows = ds(start[steps], ROWS)
            full[k, rows, :] = (
                acc[k, rows, :] + got[k, pl.ds(stage_at[steps - 1], ROWS), :].astype(jnp.float32)
            ).astype(jnp.bfloat16)
            ag_copy(k, steps - 1).start()
        else:
            b = 2 * steps - s
            rows = ds(other[b], width[b])
            pltpu.make_async_remote_copy(
                src_ref=full.at[k, rows], dst_ref=full.at[k, rows],
                send_sem=ar_send.at[k, steps + b], recv_sem=ar_recv.at[k, steps + b],
                device_id={"owner": peers[b]}, device_id_type=MESH,
            ).wait_recv()
            if b > 0:
                ag_copy(k, b - 1).start()
            else:
                out_copy(k).start()

    def turn(t, c):
        for s in range(2 * steps, -1, -1):
            k = t - s

            @pl.when((k >= 0) & (k < chunks))
            def _(k=k, s=s):
                stage(k, s)

        return c

    lax.fori_loop(0, chunks + 2 * steps, turn, 0)

    each_peer(lambda p: push_copy(p).wait())
    incoming_copy = pltpu.make_async_copy(incoming, incoming_out, out_sem.at[chunks + 1])
    incoming_copy.start()

    def drain(k, c):
        for b in range(steps):
            rs_copy(k, b).wait_send()
            ag_copy(k, b).wait_send()
        out_copy(k).wait()
        return c

    lax.fori_loop(0, chunks, drain, 0)
    result_copy.wait()
    incoming_copy.wait()


def finish_kernel(grads, incoming, hist, slots, result, grads_out, table_out, result_out):
    grads_out[...] = grads[...].astype(jnp.float32)
    result_out[...] = result[...]
    rows = table_out.shape[1]
    first = pl.program_id(0) * rows
    row_ids = lax.broadcasted_iota(jnp.int32, (rows, slots.shape[1]), 0) + first
    hit = row_ids == slots[...]
    place = jnp.where(hit, 1.0, 0.0)
    fresh = dot(place.astype(jnp.bfloat16), incoming[...])
    used = jnp.max(place, axis=1, keepdims=True)
    table_out[0] = jnp.where(used > 0, fresh, hist[0].astype(jnp.float32)).astype(jnp.bfloat16)


def body(features, history, weights, edge_weights, requests, counts, push_slots, cotangent):
    owners = lax.axis_size("owner")
    batch, hidden = features.shape
    layers, hist_rows, _ = history.shape
    slots = requests.shape[2]
    cells = owners * slots
    columns = batch + cells
    steps = owners.bit_length() - 1
    size = ROWS * owners
    chunks = layers * hidden // size
    grad_scale = 1.0 / math.sqrt(owners * batch)
    req = jnp.broadcast_to(requests[0][:, :, None], (owners, slots, 128))
    used = (jnp.arange(slots, dtype=jnp.int32)[None, :] < counts[0][:, None]).reshape(1, cells)
    valid = jnp.concatenate([jnp.ones((1, batch), jnp.float32), used.astype(jnp.float32)], axis=1)
    bf = jnp.bfloat16
    vmem = pl.BlockSpec(memory_space=pltpu.VMEM)
    hbm = pl.BlockSpec(memory_space=pl.ANY)
    dma = pltpu.SemaphoreType.DMA
    grads, incoming, result = pl.pallas_call(
        functools.partial(step_kernel, owners, slots, grad_scale),
        out_shape=(
            jax.ShapeDtypeStruct((layers * hidden, hidden), bf),
            jax.ShapeDtypeStruct((batch, hidden), bf),
            jax.ShapeDtypeStruct((batch, hidden), bf),
        ),
        in_specs=[vmem] * 7,
        out_specs=(hbm, hbm, hbm),
        scratch_shapes=[
            pltpu.VMEM((owners, slots, 128), jnp.int32),
            pltpu.VMEM((cells, hist_rows), bf),
            pltpu.VMEM((2, cells, hidden), bf),
            pltpu.VMEM((2, cells, hidden), bf),
            pltpu.VMEM((batch, columns), bf),
            pltpu.VMEM((2, batch, hidden), bf),
            pltpu.VMEM((2, batch, hidden), bf),
            pltpu.VMEM((batch, hidden), bf),
            pltpu.VMEM((batch, hidden), jnp.float32),
            pltpu.VMEM((batch, hidden), bf),
            pltpu.VMEM((batch, hidden), bf),
            pltpu.VMEM((chunks, size, hidden), jnp.float32),
            pltpu.VMEM((chunks, size, hidden), bf),
            pltpu.VMEM((chunks, size, hidden), bf),
            pltpu.VMEM((chunks, size, hidden), bf),
            dma((owners,)), dma((owners,)),
            dma((2, owners)), dma((2, owners)),
            dma((owners,)), dma((owners,)),
            dma((chunks, 2 * steps)), dma((chunks, 2 * steps)),
            dma((chunks + 2,)),
        ],
        compiler_params=pltpu.CompilerParams(
            collective_id=0, has_side_effects=True, vmem_limit_bytes=60 * MIB
        ),
    )(features, history, weights, edge_weights, valid, req, cotangent)

    parts = 8
    table_rows = hist_rows // parts
    grad_rows = layers * hidden // parts
    out_grads, table, out = pl.pallas_call(
        finish_kernel,
        grid=(parts,),
        out_shape=(
            jax.ShapeDtypeStruct((layers * hidden, hidden), jnp.float32),
            jax.ShapeDtypeStruct((1, hist_rows, hidden), bf),
            jax.ShapeDtypeStruct((batch, hidden), bf),
        ),
        in_specs=[
            pl.BlockSpec((grad_rows, hidden), lambda i: (i, 0)),
            pl.BlockSpec((batch, hidden), lambda i: (0, 0)),
            pl.BlockSpec((1, table_rows, hidden), lambda i: (1, i, 0)),
            pl.BlockSpec((1, batch), lambda i: (0, 0)),
            pl.BlockSpec((batch // parts, hidden), lambda i: (i, 0)),
        ],
        out_specs=(
            pl.BlockSpec((grad_rows, hidden), lambda i: (i, 0)),
            pl.BlockSpec((1, table_rows, hidden), lambda i: (0, i, 0)),
            pl.BlockSpec((batch // parts, hidden), lambda i: (i, 0)),
        ),
        compiler_params=pltpu.CompilerParams(vmem_limit_bytes=32 * MIB),
    )(grads, incoming, history, push_slots, result)
    return out, table, out_grads.reshape(layers, hidden, hidden)


def solution(mesh):
    in_specs = (
        P(("groups", "owner"), None),
        P(None, ("groups", "owner"), None),
        P(),
        P(("groups", "owner"), None),
        P(("groups", "owner"), None, None),
        P(("groups", "owner"), None),
        P(("groups", "owner"), None),
        P(("groups", "owner"), None),
    )
    out_specs = (
        P(("groups", "owner"), None),
        P(None, ("groups", "owner"), None),
        P("groups", None, None),
    )
    return jax.shard_map(body, mesh=mesh, in_specs=in_specs, out_specs=out_specs, check_vma=False)
```

```python
import functools
import math

import jax
import jax.numpy as jnp
from jax import lax
from jax.experimental import pallas as pl
from jax.experimental.pallas import tpu as pltpu
from jax.sharding import PartitionSpec as P

RESIDUAL = 0.1
MESH = pl.DeviceIdType.MESH
TILE = 256
ROWS = 16
SPLIT = 1
GAP = 2
MIB = 1 << 20


def strength(layer_no):
    return math.log(0.5 / (layer_no + 1) + 1.0)


def ds(start, size, unit=ROWS):
    return pl.ds(pl.multiple_of(start, unit), size)


def dot(a, b, dims=((1,), (0,))):
    return lax.dot_general(a, b, (dims, ((), ())), preferred_element_type=jnp.float32)


def step_kernel(
    owners, slots, grad_scale,
    feat_in, hist_in, weights_in, edge_in, valid, req, cot_in,
    grads_out, incoming_out, result_out,
    feat, hist, weights, edge, cot, req_in, onehot, served, pulled, adj, sup, gate, cur1, back, result, incoming,
    acc, sent, got, full,
    req_send, req_recv, pull_send, pull_recv, push_send, push_recv, ar_send, ar_recv, out_sem, in_sem,
):
    me = lax.axis_index("owner")
    batch, hidden = feat.shape
    hist_rows = hist.shape[1]
    push = batch // owners
    steps = owners.bit_length() - 1
    size = ROWS * owners
    wide = hidden // SPLIT
    half = SPLIT * hidden // size
    chunks = 2 * half
    blocks = hidden // TILE

    loads = {}
    for i, (name, src, dst) in enumerate((
        ("edge", edge_in, edge), ("hist0", hist_in.at[0], hist.at[0]),
        ("hist1", hist_in.at[1], hist.at[1]), ("feat", feat_in, feat),
        ("weights0", weights_in.at[0], weights.at[0]),
        ("weights1", weights_in.at[1], weights.at[1]), ("cot", cot_in, cot),
    )):
        loads[name] = pltpu.make_async_copy(src, dst, in_sem.at[i])
        loads[name].start()

    barrier = pltpu.get_barrier_semaphore()

    def greet(p, c):
        pl.semaphore_signal(
            barrier, inc=1, device_id={"owner": lax.rem(me + p, owners)}, device_id_type=MESH
        )
        return c

    lax.fori_loop(1, owners, greet, 0)
    pl.semaphore_wait(barrier, owners - 1)

    def req_copy(p):
        peer = lax.rem(me + p, owners)
        return pltpu.make_async_remote_copy(
            src_ref=req.at[peer], dst_ref=req_in.at[me],
            send_sem=req_send.at[p], recv_sem=req_recv.at[p],
            device_id={"owner": peer}, device_id_type=MESH,
        )

    def each_peer(fn):
        def run(p, c):
            fn(p)
            return c

        lax.fori_loop(1, owners, run, 0)

    each_peer(lambda p: req_copy(p).start())
    req_in[me] = req[me]

    loads["edge"].wait()

    def norm_rows(i, c):
        rows = ds(i * 32, 32, 32)
        masked = edge[rows, :] * valid[...]
        adj[rows, :] = (masked / jnp.sum(masked, axis=1, keepdims=True)).astype(jnp.bfloat16)
        return c

    lax.fori_loop(0, batch // 32, norm_rows, 0)
    each_peer(lambda p: req_copy(p).wait())

    def pick_rows(o, c):
        rows = ds(o * slots, slots)
        want = req_in[o]
        for j in range(hist_rows // 128):
            lanes = lax.broadcasted_iota(jnp.int32, (slots, 128), 1) + j * 128
            onehot[rows, j * 128:(j + 1) * 128] = jnp.where(lanes == want, 1.0, 0.0).astype(
                jnp.bfloat16
            )
        return c

    lax.fori_loop(0, owners, pick_rows, 0)

    def pull_copy(layer_no, p):
        peer = lax.rem(me + p, owners)
        return pltpu.make_async_remote_copy(
            src_ref=served.at[layer_no, ds(peer * slots, slots)],
            dst_ref=pulled.at[layer_no, ds(me * slots, slots)],
            send_sem=pull_send.at[layer_no, p], recv_sem=pull_recv.at[layer_no, p],
            device_id={"owner": peer}, device_id_type=MESH,
        )

    def serve(layer_no):
        loads[f"hist{layer_no}"].wait()

        def pick(j, c):
            cols = ds(j * TILE, TILE, TILE)
            served[layer_no, :, cols] = dot(onehot[...], hist[layer_no, :, cols]).astype(jnp.bfloat16)
            return c

        lax.fori_loop(0, blocks, pick, 0)
        pulled[layer_no, ds(me * slots, slots), :] = served[layer_no, ds(me * slots, slots), :]

    serve(0)
    each_peer(lambda p: pull_copy(0, p).start())
    serve(1)

    def push_copy(p):
        peer = lax.rem(me + p, owners)
        return pltpu.make_async_remote_copy(
            src_ref=cur1.at[ds(peer * push, push)],
            dst_ref=incoming.at[ds(me * push, push)],
            send_sem=push_send.at[p], recv_sem=push_recv.at[p],
            device_id={"owner": peer}, device_id_type=MESH,
        )

    for layer_no in range(2):
        mix = strength(layer_no)
        source = feat if layer_no == 0 else cur1
        if layer_no == 0:
            loads["feat"].wait()

        def own_sum(j, c, source=source):
            cols = ds(j * TILE, TILE, TILE)
            back[:, cols] = dot(adj[:, :batch], source[:, cols])
            return c

        lax.fori_loop(0, blocks, own_sum, 0)
        each_peer(lambda p, layer_no=layer_no: pull_copy(layer_no, p).wait())
        if layer_no == 0:
            each_peer(lambda p: pull_copy(1, p).start())
        else:
            each_peer(lambda p: push_copy(p).start())

        def far_sum(j, c, layer_no=layer_no):
            cols = ds(j * TILE, TILE, TILE)
            total = back[:, cols] + dot(adj[:, batch:], pulled[layer_no, :, cols])
            sup[layer_no, :, cols] = (
                (1.0 - RESIDUAL) * total + RESIDUAL * feat[:, cols].astype(jnp.float32)
            ).astype(jnp.bfloat16)
            return c

        lax.fori_loop(0, blocks, far_sum, 0)
        loads[f"weights{layer_no}"].wait()
        if layer_no == 1:
            loads["cot"].wait()

        def linear(j, c, layer_no=layer_no, mix=mix):
            cols = ds(j * TILE, TILE, TILE)
            pre = (1.0 - mix) * sup[layer_no, :, cols].astype(jnp.float32) + mix * dot(
                sup[layer_no], weights[layer_no, :, cols]
            )
            out = jnp.maximum(pre, 0.0).astype(jnp.bfloat16)
            if layer_no == 0:
                cur1[:, cols] = out
            else:
                result[:, cols] = out
                gate[1, :, cols] = jnp.where(
                    pre > 0, cot[:, cols].astype(jnp.float32), 0.0
                ).astype(jnp.bfloat16)
            return c

        lax.fori_loop(0, blocks, linear, 0)
        if layer_no == 0:
            incoming[ds(me * push, push), :] = cur1[ds(me * push, push), :]

    result_copy = pltpu.make_async_copy(result, result_out, out_sem.at[chunks])
    result_copy.start()

    def backward():
        mix = strength(1)

        def through(j, c):
            cols = ds(j * TILE, TILE, TILE)
            value = (1.0 - mix) * gate[1, :, cols].astype(jnp.float32) + mix * dot(
                gate[1], weights[1, cols, :], ((1,), (1,))
            )
            gate[0, :, cols] = value.astype(jnp.bfloat16)
            return c

        lax.fori_loop(0, blocks, through, 0)

        def up(j, c):
            cols = ds(j * TILE, TILE, TILE)
            upstream = (1.0 - RESIDUAL) * dot(adj[:, :batch], gate[0, :, cols], ((0,), (0,)))
            gate[0, :, cols] = jnp.where(
                cur1[:, cols].astype(jnp.float32) > 0, upstream, 0.0
            ).astype(jnp.bfloat16)
            return c

        lax.fori_loop(0, blocks, up, 0)

    bits = [lax.rem(me // (1 << b), 2) for b in range(steps)]
    peers = [me + (1 - 2 * bits[b]) * (1 << b) for b in range(steps)]
    width = [size >> (b + 1) for b in range(steps)]
    start = [0]
    for b in range(steps):
        start.append(start[-1] + bits[b] * width[b])
    other = [start[b] + (1 - bits[b]) * width[b] for b in range(steps)]
    stage_at = [size - (size >> b) for b in range(steps)]

    def rs_copy(k, b):
        rows = pl.ds(stage_at[b], width[b])
        return pltpu.make_async_remote_copy(
            src_ref=sent.at[k, rows], dst_ref=got.at[k, rows],
            send_sem=ar_send.at[k, b], recv_sem=ar_recv.at[k, b],
            device_id={"owner": peers[b]}, device_id_type=MESH,
        )

    def ag_copy(k, b):
        rows = ds(start[b + 1], width[b])
        return pltpu.make_async_remote_copy(
            src_ref=full.at[k, rows], dst_ref=full.at[k, rows],
            send_sem=ar_send.at[k, steps + b], recv_sem=ar_recv.at[k, steps + b],
            device_id={"owner": peers[b]}, device_id_type=MESH,
        )

    def out_copy(k):
        row = (1 - k // half) * hidden + lax.rem(k, half) // SPLIT * size
        cols = ds(lax.rem(k, SPLIT) * wide, wide, 128)
        return pltpu.make_async_copy(
            full.at[k], grads_out.at[ds(row, size), cols], out_sem.at[k]
        )

    def each_row(count, fn):
        def run(i, c):
            fn(i * ROWS)
            return c

        lax.fori_loop(0, count // ROWS, run, 0)

    def stage(k, s):
        if s == 0:
            @pl.when(k == half)
            def _():
                backward()

            layer_no = 1 - k // half
            scale = grad_scale * jnp.where(layer_no == 1, strength(1), strength(0))

            def product(i, c):
                rows = ds(lax.rem(k, half) // SPLIT * size + i * TILE, TILE, TILE)
                cols = ds(lax.rem(k, SPLIT) * wide, wide, 128)
                acc[k, ds(i * TILE, TILE, TILE), :] = scale * dot(
                    sup[layer_no, :, rows], gate[layer_no, :, cols], ((0,), (0,))
                )
                return c

            lax.fori_loop(0, size // TILE, product, 0)

            def pack(i):
                sent[k, ds(i, ROWS), :] = acc[k, ds(other[0] + i, ROWS), :].astype(jnp.bfloat16)

            each_row(width[0], pack)
            rs_copy(k, 0).start()
        elif s < steps:
            rs_copy(k, s - 1).wait_recv()
            base = stage_at[s - 1]

            def pack(i):
                total = acc[k, ds(other[s] + i, ROWS), :] + got[
                    k, ds(base + (1 - bits[s]) * width[s] + i, ROWS), :
                ].astype(jnp.float32)
                sent[k, ds(stage_at[s] + i, ROWS), :] = total.astype(jnp.bfloat16)

            each_row(width[s], pack)
            rs_copy(k, s).start()

            def keep(i):
                rows = ds(start[s + 1] + i, ROWS)
                acc[k, rows, :] = acc[k, rows, :] + got[
                    k, ds(base + bits[s] * width[s] + i, ROWS), :
                ].astype(jnp.float32)

            each_row(width[s], keep)
        elif s == steps:
            rs_copy(k, s - 1).wait_recv()
            rows = ds(start[steps], ROWS)
            full[k, rows, :] = (
                acc[k, rows, :] + got[k, pl.ds(stage_at[steps - 1], ROWS), :].astype(jnp.float32)
            ).astype(jnp.bfloat16)
            ag_copy(k, steps - 1).start()
        else:
            b = 2 * steps - s
            rows = ds(other[b], width[b])
            pltpu.make_async_remote_copy(
                src_ref=full.at[k, rows], dst_ref=full.at[k, rows],
                send_sem=ar_send.at[k, steps + b], recv_sem=ar_recv.at[k, steps + b],
                device_id={"owner": peers[b]}, device_id_type=MESH,
            ).wait_recv()
            if b > 0:
                ag_copy(k, b - 1).start()
            else:
                out_copy(k).start()

    def turn(t, c):
        for s in range(2 * steps, -1, -1):
            k = t - GAP * s

            @pl.when((k >= 0) & (k < chunks))
            def _(k=k, s=s):
                stage(k, s)

        return c

    lax.fori_loop(0, chunks + GAP * 2 * steps, turn, 0)

    each_peer(lambda p: push_copy(p).wait())
    incoming_copy = pltpu.make_async_copy(incoming, incoming_out, out_sem.at[chunks + 1])
    incoming_copy.start()

    def drain(k, c):
        for b in range(steps):
            rs_copy(k, b).wait_send()
            ag_copy(k, b).wait_send()
        out_copy(k).wait()
        return c

    lax.fori_loop(0, chunks, drain, 0)
    result_copy.wait()
    incoming_copy.wait()


def finish_kernel(grads, incoming, hist, slots, result, grads_out, table_out, result_out):
    grads_out[...] = grads[...].astype(jnp.float32)
    result_out[...] = result[...]
    rows = table_out.shape[1]
    first = pl.program_id(0) * rows
    row_ids = lax.broadcasted_iota(jnp.int32, (rows, slots.shape[1]), 0) + first
    hit = row_ids == slots[...]
    place = jnp.where(hit, 1.0, 0.0)
    fresh = dot(place.astype(jnp.bfloat16), incoming[...])
    used = jnp.max(place, axis=1, keepdims=True)
    table_out[0] = jnp.where(used > 0, fresh, hist[0].astype(jnp.float32)).astype(jnp.bfloat16)


def body(features, history, weights, edge_weights, requests, counts, push_slots, cotangent):
    owners = lax.axis_size("owner")
    batch, hidden = features.shape
    layers, hist_rows, _ = history.shape
    slots = requests.shape[2]
    cells = owners * slots
    columns = batch + cells
    steps = owners.bit_length() - 1
    size = ROWS * owners
    chunks = SPLIT * layers * hidden // size
    wide = hidden // SPLIT
    grad_scale = 1.0 / math.sqrt(owners * batch)
    req = jnp.broadcast_to(requests[0][:, :, None], (owners, slots, 128))
    used = (jnp.arange(slots, dtype=jnp.int32)[None, :] < counts[0][:, None]).reshape(1, cells)
    valid = jnp.concatenate([jnp.ones((1, batch), jnp.float32), used.astype(jnp.float32)], axis=1)
    bf = jnp.bfloat16
    vmem = pl.BlockSpec(memory_space=pltpu.VMEM)
    hbm = pl.BlockSpec(memory_space=pl.ANY)
    dma = pltpu.SemaphoreType.DMA
    grads, incoming, result = pl.pallas_call(
        functools.partial(step_kernel, owners, slots, grad_scale),
        out_shape=(
            jax.ShapeDtypeStruct((layers * hidden, hidden), bf),
            jax.ShapeDtypeStruct((batch, hidden), bf),
            jax.ShapeDtypeStruct((batch, hidden), bf),
        ),
        in_specs=[hbm] * 4 + [vmem] * 2 + [hbm],
        out_specs=(hbm, hbm, hbm),
        scratch_shapes=[
            pltpu.VMEM((batch, hidden), bf),
            pltpu.VMEM((layers, hist_rows, hidden), bf),
            pltpu.VMEM((layers, hidden, hidden), bf),
            pltpu.VMEM((batch, columns), jnp.float32),
            pltpu.VMEM((batch, hidden), bf),
            pltpu.VMEM((owners, slots, 128), jnp.int32),
            pltpu.VMEM((cells, hist_rows), bf),
            pltpu.VMEM((2, cells, hidden), bf),
            pltpu.VMEM((2, cells, hidden), bf),
            pltpu.VMEM((batch, columns), bf),
            pltpu.VMEM((2, batch, hidden), bf),
            pltpu.VMEM((2, batch, hidden), bf),
            pltpu.VMEM((batch, hidden), bf),
            pltpu.VMEM((batch, hidden), jnp.float32),
            pltpu.VMEM((batch, hidden), bf),
            pltpu.VMEM((batch, hidden), bf),
            pltpu.VMEM((chunks, size, wide), jnp.float32),
            pltpu.VMEM((chunks, size, wide), bf),
            pltpu.VMEM((chunks, size, wide), bf),
            pltpu.VMEM((chunks, size, wide), bf),
            dma((owners,)), dma((owners,)),
            dma((2, owners)), dma((2, owners)),
            dma((owners,)), dma((owners,)),
            dma((chunks, 2 * steps)), dma((chunks, 2 * steps)),
            dma((chunks + 2,)),
            dma((7,)),
        ],
        compiler_params=pltpu.CompilerParams(
            collective_id=0, has_side_effects=True, vmem_limit_bytes=60 * MIB
        ),
    )(features, history, weights, edge_weights, valid, req, cotangent)

    parts = 4
    table_rows = hist_rows // parts
    grad_rows = layers * hidden // parts
    out_grads, table, out = pl.pallas_call(
        finish_kernel,
        grid=(parts,),
        out_shape=(
            jax.ShapeDtypeStruct((layers * hidden, hidden), jnp.float32),
            jax.ShapeDtypeStruct((1, hist_rows, hidden), bf),
            jax.ShapeDtypeStruct((batch, hidden), bf),
        ),
        in_specs=[
            pl.BlockSpec((grad_rows, hidden), lambda i: (i, 0)),
            pl.BlockSpec((batch, hidden), lambda i: (0, 0)),
            pl.BlockSpec((1, table_rows, hidden), lambda i: (1, i, 0)),
            pl.BlockSpec((1, batch), lambda i: (0, 0)),
            pl.BlockSpec((batch // parts, hidden), lambda i: (i, 0)),
        ],
        out_specs=(
            pl.BlockSpec((grad_rows, hidden), lambda i: (i, 0)),
            pl.BlockSpec((1, table_rows, hidden), lambda i: (0, i, 0)),
            pl.BlockSpec((batch // parts, hidden), lambda i: (i, 0)),
        ),
        compiler_params=pltpu.CompilerParams(vmem_limit_bytes=60 * MIB),
    )(grads, incoming, history, push_slots, result)
    return out, table, out_grads.reshape(layers, hidden, hidden)


def solution(mesh):
    in_specs = (
        P(("groups", "owner"), None),
        P(None, ("groups", "owner"), None),
        P(),
        P(("groups", "owner"), None),
        P(("groups", "owner"), None, None),
        P(("groups", "owner"), None),
        P(("groups", "owner"), None),
        P(("groups", "owner"), None),
    )
    out_specs = (
        P(("groups", "owner"), None),
        P(None, ("groups", "owner"), None),
        P("groups", None, None),
    )
    return jax.shard_map(body, mesh=mesh, in_specs=in_specs, out_specs=out_specs, check_vma=False)
```

```python
import functools
import math

import jax
import jax.numpy as jnp
from jax import lax
from jax.experimental import pallas as pl
from jax.experimental.pallas import tpu as pltpu
from jax.sharding import PartitionSpec as P

RESIDUAL = 0.1
MESH = pl.DeviceIdType.MESH
TILE = 256
ROWS = 16
SPLIT = 1
GAP = 2
MIB = 1 << 20


def strength(layer_no):
    return math.log(0.5 / (layer_no + 1) + 1.0)


def ds(start, size, unit=ROWS):
    return pl.ds(pl.multiple_of(start, unit), size)


def dot(a, b, dims=((1,), (0,))):
    return lax.dot_general(a, b, (dims, ((), ())), preferred_element_type=jnp.float32)


def step_kernel(
    owners, slots, grad_scale,
    feat_in, hist_in, weights_in, edge_in, valid, req, cot_in,
    grads_out, incoming_out, result_out,
    feat, hist, weights, edge, cot, req_in, onehot, served, pulled, adj, sup, gate, cur1, back, result, incoming,
    acc, sent, got, full,
    req_send, req_recv, pull_send, pull_recv, push_send, push_recv, ar_send, ar_recv, out_sem, in_sem,
):
    me = lax.axis_index("owner")
    batch, hidden = feat.shape
    hist_rows = hist.shape[1]
    push = batch // owners
    steps = owners.bit_length() - 1
    size = ROWS * owners
    wide = hidden // SPLIT
    half = SPLIT * hidden // size
    chunks = 2 * half
    blocks = hidden // TILE

    loads = {}
    for i, (name, src, dst) in enumerate((
        ("edge", edge_in, edge), ("hist0", hist_in.at[0], hist.at[0]),
        ("hist1", hist_in.at[1], hist.at[1]), ("feat", feat_in, feat),
        ("weights0", weights_in.at[0], weights.at[0]),
        ("weights1", weights_in.at[1], weights.at[1]), ("cot", cot_in, cot),
    )):
        loads[name] = pltpu.make_async_copy(src, dst, in_sem.at[i])
        loads[name].start()

    barrier = pltpu.get_barrier_semaphore()

    def greet(p, c):
        pl.semaphore_signal(
            barrier, inc=1, device_id={"owner": lax.rem(me + p, owners)}, device_id_type=MESH
        )
        return c

    lax.fori_loop(1, owners, greet, 0)
    pl.semaphore_wait(barrier, owners - 1)

    def req_copy(p):
        peer = lax.rem(me + p, owners)
        return pltpu.make_async_remote_copy(
            src_ref=req.at[peer], dst_ref=req_in.at[me],
            send_sem=req_send.at[p], recv_sem=req_recv.at[p],
            device_id={"owner": peer}, device_id_type=MESH,
        )

    def each_peer(fn):
        def run(p, c):
            fn(p)
            return c

        lax.fori_loop(1, owners, run, 0)

    each_peer(lambda p: req_copy(p).start())
    req_in[me] = req[me]

    loads["edge"].wait()

    def norm_rows(i, c):
        rows = ds(i * 32, 32, 32)
        masked = edge[rows, :] * valid[...]
        adj[rows, :] = (masked / jnp.sum(masked, axis=1, keepdims=True)).astype(jnp.bfloat16)
        return c

    lax.fori_loop(0, batch // 32, norm_rows, 0)
    each_peer(lambda p: req_copy(p).wait())

    def pick_rows(o, c):
        rows = ds(o * slots, slots)
        want = req_in[o]
        for j in range(hist_rows // 128):
            lanes = lax.broadcasted_iota(jnp.int32, (slots, 128), 1) + j * 128
            onehot[rows, j * 128:(j + 1) * 128] = jnp.where(lanes == want, 1.0, 0.0).astype(
                jnp.bfloat16
            )
        return c

    lax.fori_loop(0, owners, pick_rows, 0)

    def pull_copy(layer_no, p):
        peer = lax.rem(me + p, owners)
        return pltpu.make_async_remote_copy(
            src_ref=served.at[layer_no, ds(peer * slots, slots)],
            dst_ref=pulled.at[layer_no, ds(me * slots, slots)],
            send_sem=pull_send.at[layer_no, p], recv_sem=pull_recv.at[layer_no, p],
            device_id={"owner": peer}, device_id_type=MESH,
        )

    def serve(layer_no):
        loads[f"hist{layer_no}"].wait()

        def pick(j, c):
            cols = ds(j * TILE, TILE, TILE)
            served[layer_no, :, cols] = dot(onehot[...], hist[layer_no, :, cols]).astype(jnp.bfloat16)
            return c

        lax.fori_loop(0, blocks, pick, 0)
        pulled[layer_no, ds(me * slots, slots), :] = served[layer_no, ds(me * slots, slots), :]

    serve(0)
    each_peer(lambda p: pull_copy(0, p).start())
    serve(1)
    each_peer(lambda p: pull_copy(1, p).start())

    def push_copy(p):
        peer = lax.rem(me + p, owners)
        return pltpu.make_async_remote_copy(
            src_ref=cur1.at[ds(peer * push, push)],
            dst_ref=incoming.at[ds(me * push, push)],
            send_sem=push_send.at[p], recv_sem=push_recv.at[p],
            device_id={"owner": peer}, device_id_type=MESH,
        )

    for layer_no in range(2):
        mix = strength(layer_no)
        source = feat if layer_no == 0 else cur1
        if layer_no == 0:
            loads["feat"].wait()

        def own_sum(j, c, source=source):
            cols = ds(j * TILE, TILE, TILE)
            back[:, cols] = dot(adj[:, :batch], source[:, cols])
            return c

        lax.fori_loop(0, blocks, own_sum, 0)
        each_peer(lambda p, layer_no=layer_no: pull_copy(layer_no, p).wait())
        if layer_no == 1:
            each_peer(lambda p: push_copy(p).start())

        def far_sum(j, c, layer_no=layer_no):
            cols = ds(j * TILE, TILE, TILE)
            total = back[:, cols] + dot(adj[:, batch:], pulled[layer_no, :, cols])
            sup[layer_no, :, cols] = (
                (1.0 - RESIDUAL) * total + RESIDUAL * feat[:, cols].astype(jnp.float32)
            ).astype(jnp.bfloat16)
            return c

        lax.fori_loop(0, blocks, far_sum, 0)
        loads[f"weights{layer_no}"].wait()
        if layer_no == 1:
            loads["cot"].wait()

        def linear(j, c, layer_no=layer_no, mix=mix):
            cols = ds(j * TILE, TILE, TILE)
            pre = (1.0 - mix) * sup[layer_no, :, cols].astype(jnp.float32) + mix * dot(
                sup[layer_no], weights[layer_no, :, cols]
            )
            out = jnp.maximum(pre, 0.0).astype(jnp.bfloat16)
            if layer_no == 0:
                cur1[:, cols] = out
            else:
                result[:, cols] = out
                gate[1, :, cols] = jnp.where(
                    pre > 0, cot[:, cols].astype(jnp.float32), 0.0
                ).astype(jnp.bfloat16)
            return c

        lax.fori_loop(0, blocks, linear, 0)
        if layer_no == 0:
            incoming[ds(me * push, push), :] = cur1[ds(me * push, push), :]

    result_copy = pltpu.make_async_copy(result, result_out, out_sem.at[chunks])
    result_copy.start()

    def backward():
        mix = strength(1)

        def through(j, c):
            cols = ds(j * TILE, TILE, TILE)
            value = (1.0 - mix) * gate[1, :, cols].astype(jnp.float32) + mix * dot(
                gate[1], weights[1, cols, :], ((1,), (1,))
            )
            gate[0, :, cols] = value.astype(jnp.bfloat16)
            return c

        lax.fori_loop(0, blocks, through, 0)

        def up(j, c):
            cols = ds(j * TILE, TILE, TILE)
            upstream = (1.0 - RESIDUAL) * dot(adj[:, :batch], gate[0, :, cols], ((0,), (0,)))
            gate[0, :, cols] = jnp.where(
                cur1[:, cols].astype(jnp.float32) > 0, upstream, 0.0
            ).astype(jnp.bfloat16)
            return c

        lax.fori_loop(0, blocks, up, 0)

    bits = [lax.rem(me // (1 << b), 2) for b in range(steps)]
    peers = [me + (1 - 2 * bits[b]) * (1 << b) for b in range(steps)]
    width = [size >> (b + 1) for b in range(steps)]
    start = [0]
    for b in range(steps):
        start.append(start[-1] + bits[b] * width[b])
    other = [start[b] + (1 - bits[b]) * width[b] for b in range(steps)]
    stage_at = [size - (size >> b) for b in range(steps)]

    def rs_copy(k, b):
        rows = pl.ds(stage_at[b], width[b])
        return pltpu.make_async_remote_copy(
            src_ref=sent.at[k, rows], dst_ref=got.at[k, rows],
            send_sem=ar_send.at[k, b], recv_sem=ar_recv.at[k, b],
            device_id={"owner": peers[b]}, device_id_type=MESH,
        )

    def ag_copy(k, b):
        rows = ds(start[b + 1], width[b])
        return pltpu.make_async_remote_copy(
            src_ref=full.at[k, rows], dst_ref=full.at[k, rows],
            send_sem=ar_send.at[k, steps + b], recv_sem=ar_recv.at[k, steps + b],
            device_id={"owner": peers[b]}, device_id_type=MESH,
        )

    def out_copy(k):
        row = (1 - k // half) * hidden + lax.rem(k, half) // SPLIT * size
        cols = ds(lax.rem(k, SPLIT) * wide, wide, 128)
        return pltpu.make_async_copy(
            full.at[k], grads_out.at[ds(row, size), cols], out_sem.at[k]
        )

    def each_row(count, fn):
        def run(i, c):
            fn(i * ROWS)
            return c

        lax.fori_loop(0, count // ROWS, run, 0)

    def stage(k, s):
        if s == 0:
            @pl.when(k == half)
            def _():
                backward()

            layer_no = 1 - k // half
            scale = grad_scale * jnp.where(layer_no == 1, strength(1), strength(0))

            def product(i, c):
                rows = ds(lax.rem(k, half) // SPLIT * size + i * TILE, TILE, TILE)
                cols = ds(lax.rem(k, SPLIT) * wide, wide, 128)
                acc[k, ds(i * TILE, TILE, TILE), :] = scale * dot(
                    sup[layer_no, :, rows], gate[layer_no, :, cols], ((0,), (0,))
                )
                return c

            lax.fori_loop(0, size // TILE, product, 0)

            def pack(i):
                sent[k, ds(i, ROWS), :] = acc[k, ds(other[0] + i, ROWS), :].astype(jnp.bfloat16)

            each_row(width[0], pack)
            rs_copy(k, 0).start()
        elif s < steps:
            rs_copy(k, s - 1).wait_recv()
            base = stage_at[s - 1]

            def pack(i):
                total = acc[k, ds(other[s] + i, ROWS), :] + got[
                    k, ds(base + (1 - bits[s]) * width[s] + i, ROWS), :
                ].astype(jnp.float32)
                sent[k, ds(stage_at[s] + i, ROWS), :] = total.astype(jnp.bfloat16)

            each_row(width[s], pack)
            rs_copy(k, s).start()

            def keep(i):
                rows = ds(start[s + 1] + i, ROWS)
                acc[k, rows, :] = acc[k, rows, :] + got[
                    k, ds(base + bits[s] * width[s] + i, ROWS), :
                ].astype(jnp.float32)

            each_row(width[s], keep)
        elif s == steps:
            rs_copy(k, s - 1).wait_recv()
            rows = ds(start[steps], ROWS)
            full[k, rows, :] = (
                acc[k, rows, :] + got[k, pl.ds(stage_at[steps - 1], ROWS), :].astype(jnp.float32)
            ).astype(jnp.bfloat16)
            ag_copy(k, steps - 1).start()
        else:
            b = 2 * steps - s
            rows = ds(other[b], width[b])
            pltpu.make_async_remote_copy(
                src_ref=full.at[k, rows], dst_ref=full.at[k, rows],
                send_sem=ar_send.at[k, steps + b], recv_sem=ar_recv.at[k, steps + b],
                device_id={"owner": peers[b]}, device_id_type=MESH,
            ).wait_recv()
            if b > 0:
                ag_copy(k, b - 1).start()
            else:
                out_copy(k).start()

    def turn(t, c):
        for s in range(2 * steps, -1, -1):
            k = t - GAP * s

            @pl.when((k >= 0) & (k < chunks))
            def _(k=k, s=s):
                stage(k, s)

        return c

    lax.fori_loop(0, chunks + GAP * 2 * steps, turn, 0)

    each_peer(lambda p: push_copy(p).wait())
    incoming_copy = pltpu.make_async_copy(incoming, incoming_out, out_sem.at[chunks + 1])
    incoming_copy.start()

    def drain(k, c):
        for b in range(steps):
            rs_copy(k, b).wait_send()
            ag_copy(k, b).wait_send()
        out_copy(k).wait()
        return c

    lax.fori_loop(0, chunks, drain, 0)
    result_copy.wait()
    incoming_copy.wait()


def finish_kernel(grads, incoming, hist, slots, result, grads_out, table_out, result_out):
    grads_out[...] = grads[...].astype(jnp.float32)
    result_out[...] = result[...]
    rows = table_out.shape[1]
    first = pl.program_id(0) * rows
    row_ids = lax.broadcasted_iota(jnp.int32, (rows, slots.shape[1]), 0) + first
    hit = row_ids == slots[...]
    place = jnp.where(hit, 1.0, 0.0)
    fresh = dot(place.astype(jnp.bfloat16), incoming[...])
    used = jnp.max(place, axis=1, keepdims=True)
    table_out[0] = jnp.where(used > 0, fresh, hist[0].astype(jnp.float32)).astype(jnp.bfloat16)


def body(features, history, weights, edge_weights, requests, counts, push_slots, cotangent):
    owners = lax.axis_size("owner")
    batch, hidden = features.shape
    layers, hist_rows, _ = history.shape
    slots = requests.shape[2]
    cells = owners * slots
    columns = batch + cells
    steps = owners.bit_length() - 1
    size = ROWS * owners
    chunks = SPLIT * layers * hidden // size
    wide = hidden // SPLIT
    grad_scale = 1.0 / math.sqrt(owners * batch)
    req = jnp.broadcast_to(requests[0][:, :, None], (owners, slots, 128))
    used = (jnp.arange(slots, dtype=jnp.int32)[None, :] < counts[0][:, None]).reshape(1, cells)
    valid = jnp.concatenate([jnp.ones((1, batch), jnp.float32), used.astype(jnp.float32)], axis=1)
    bf = jnp.bfloat16
    vmem = pl.BlockSpec(memory_space=pltpu.VMEM)
    hbm = pl.BlockSpec(memory_space=pl.ANY)
    dma = pltpu.SemaphoreType.DMA
    grads, incoming, result = pl.pallas_call(
        functools.partial(step_kernel, owners, slots, grad_scale),
        out_shape=(
            jax.ShapeDtypeStruct((layers * hidden, hidden), bf),
            jax.ShapeDtypeStruct((batch, hidden), bf),
            jax.ShapeDtypeStruct((batch, hidden), bf),
        ),
        in_specs=[hbm] * 4 + [vmem] * 2 + [hbm],
        out_specs=(hbm, hbm, hbm),
        scratch_shapes=[
            pltpu.VMEM((batch, hidden), bf),
            pltpu.VMEM((layers, hist_rows, hidden), bf),
            pltpu.VMEM((layers, hidden, hidden), bf),
            pltpu.VMEM((batch, columns), jnp.float32),
            pltpu.VMEM((batch, hidden), bf),
            pltpu.VMEM((owners, slots, 128), jnp.int32),
            pltpu.VMEM((cells, hist_rows), bf),
            pltpu.VMEM((2, cells, hidden), bf),
            pltpu.VMEM((2, cells, hidden), bf),
            pltpu.VMEM((batch, columns), bf),
            pltpu.VMEM((2, batch, hidden), bf),
            pltpu.VMEM((2, batch, hidden), bf),
            pltpu.VMEM((batch, hidden), bf),
            pltpu.VMEM((batch, hidden), jnp.float32),
            pltpu.VMEM((batch, hidden), bf),
            pltpu.VMEM((batch, hidden), bf),
            pltpu.VMEM((chunks, size, wide), jnp.float32),
            pltpu.VMEM((chunks, size, wide), bf),
            pltpu.VMEM((chunks, size, wide), bf),
            pltpu.VMEM((chunks, size, wide), bf),
            dma((owners,)), dma((owners,)),
            dma((2, owners)), dma((2, owners)),
            dma((owners,)), dma((owners,)),
            dma((chunks, 2 * steps)), dma((chunks, 2 * steps)),
            dma((chunks + 2,)),
            dma((7,)),
        ],
        compiler_params=pltpu.CompilerParams(
            collective_id=0, has_side_effects=True, vmem_limit_bytes=60 * MIB
        ),
    )(features, history, weights, edge_weights, valid, req, cotangent)

    parts = 4
    table_rows = hist_rows // parts
    grad_rows = layers * hidden // parts
    out_grads, table, out = pl.pallas_call(
        finish_kernel,
        grid=(parts,),
        out_shape=(
            jax.ShapeDtypeStruct((layers * hidden, hidden), jnp.float32),
            jax.ShapeDtypeStruct((1, hist_rows, hidden), bf),
            jax.ShapeDtypeStruct((batch, hidden), bf),
        ),
        in_specs=[
            pl.BlockSpec((grad_rows, hidden), lambda i: (i, 0)),
            pl.BlockSpec((batch, hidden), lambda i: (0, 0)),
            pl.BlockSpec((1, table_rows, hidden), lambda i: (1, i, 0)),
            pl.BlockSpec((1, batch), lambda i: (0, 0)),
            pl.BlockSpec((batch // parts, hidden), lambda i: (i, 0)),
        ],
        out_specs=(
            pl.BlockSpec((grad_rows, hidden), lambda i: (i, 0)),
            pl.BlockSpec((1, table_rows, hidden), lambda i: (0, i, 0)),
            pl.BlockSpec((batch // parts, hidden), lambda i: (i, 0)),
        ),
        compiler_params=pltpu.CompilerParams(vmem_limit_bytes=60 * MIB),
    )(grads, incoming, history, push_slots, result)
    return out, table, out_grads.reshape(layers, hidden, hidden)


def solution(mesh):
    in_specs = (
        P(("groups", "owner"), None),
        P(None, ("groups", "owner"), None),
        P(),
        P(("groups", "owner"), None),
        P(("groups", "owner"), None, None),
        P(("groups", "owner"), None),
        P(("groups", "owner"), None),
        P(("groups", "owner"), None),
    )
    out_specs = (
        P(("groups", "owner"), None),
        P(None, ("groups", "owner"), None),
        P("groups", None, None),
    )
    return jax.shard_map(body, mesh=mesh, in_specs=in_specs, out_specs=out_specs, check_vma=False)
```
